32 devices in a mesh: kv: 8 (over y, x, core), seq: 4 (over z).
Axes of the slice: x: 2, y: 2, z: 4, core: 2. Of those that a mesh axis runs over, the one named last changes fastest.
Arguments:
- prefill_keys: bfloat16 [65536, 1024], P(('kv', 'seq')), may hold values from -50 to 50
- queries: bfloat16 [512, 8192], P('seq'), may hold values from -6 to 6
- outlier_spans: int32 [128], P(('kv', 'seq')), may hold values from 0 to 255
- start_basis: float32 [160, 1024], replicated, may hold values from -6 to 6
Outputs:
- basis: float32 [160, 1024], replicated
- coefficients: bfloat16 [160, 65536], P(None, ('kv', 'seq'))
- landmark_scores: bfloat16 [8, 512, 8192], P(None, 'seq', 'kv')
- outlier_scores: bfloat16 [8, 512, 1024], P(None, 'seq', 'kv')
The draws below stay inside these ranges and needn't reach their ends.
Inputs may be any that keep to these rules, and one draw needn't show every extreme that they name: `outlier_spans`: entries index spans of 8 rows among the rows held by the same device.
All inputs are finite; a program needn't handle non-finite values.
Results may differ from the reference program's by a relative error of at most 0.0037.
Values may be sent and summed in bfloat16 or wider, within the bound.
A program may use at most 128 MiB of HBM per device.

```python
import math
import jax
import jax.numpy as jnp
from jax import lax

KVH = 8
HEAD = 128
GROUP = 8
D = 1024
RANK = 160
ITERS = 8
SPAN = 8
OUT_DEV = 4
QROWS = 128
ROWS_DEV = 2048
TOKENS = 65536
NCHUNK = 8192
NOUT = 128
NQ = 512


def draw_prefill_keys(key, part):
    key_latent, key_mixing, key_noise, key_column, key_row = jax.random.split(jax.random.fold_in(key, 17), 5)
    latent_width = RANK * 6 // 5
    position = jnp.arange(latent_width).astype(jnp.float32)
    strength = 3.0 / (1.0 + position * 8.0 / RANK)
    mixing = jax.random.normal(key_mixing, (latent_width, D), jnp.float32) / jnp.sqrt(jnp.float32(latent_width))
    column_scale = jnp.exp(jax.random.uniform(key_column, (D,), jnp.float32, -0.7, 0.7))
    latent = jnp.clip(jax.random.normal(key_latent, (TOKENS, latent_width), jnp.float32), -5.0, 5.0)
    noise = 0.15 * jnp.clip(jax.random.normal(key_noise, (TOKENS, D), jnp.float32), -5.0, 5.0)
    row_scale = jnp.exp(jax.random.uniform(key_row, (TOKENS, 1), jnp.float32, -1.15, 1.15))
    shaped = jnp.dot(latent * strength, mixing, precision=lax.Precision.HIGHEST, preferred_element_type=jnp.float32)
    keys = (shaped + noise) * column_scale * row_scale
    return jnp.clip(keys, -48.0, 48.0).astype(jnp.bfloat16)


def touch_ends(result, own_key, least, largest):
    spot = [jax.random.randint(jax.random.fold_in(own_key, axis), (), 0, length) for axis, length in enumerate(result.shape)]
    main_axis = result.shape.index(max(result.shape))
    beside = spot[:main_axis] + [(spot[main_axis] + 1) % result.shape[main_axis]] + spot[main_axis + 1:]
    return result.at[tuple(spot)].set(least).at[tuple(beside)].set(largest)


def levels(rng, shape, cuts, least, top_value):
    loudness = 1.0
    for axis_at, shards_of in cuts:
        steps = jax.random.uniform(jax.random.fold_in(jax.random.fold_in(rng, 6), axis_at), (shards_of,), jnp.float32, least / len(cuts), top_value / len(cuts))
        loudness = loudness * jnp.repeat(jnp.exp(steps), shape[axis_at] // shards_of).reshape((-1,) + (1,) * (len(shape) - 1 - axis_at))
    return loudness


def gaussian(own_key, extent, deviation, bound, cuts=(), held_as=jnp.bfloat16):
    loudness = levels(own_key, extent, cuts, -0.22, 0.18) if cuts else 1.0
    drawn = jax.random.normal(own_key, extent, jnp.float32) * deviation * loudness
    return jnp.minimum(jnp.maximum(drawn, -bound), bound).astype(held_as)


def setup_inputs(seed: int = 0) -> dict:
    key_list = jax.random.split(jax.random.key(seed), 5)
    return {
        "prefill_keys": draw_prefill_keys(jax.random.fold_in(key_list[4], 71), 0),
        "queries": gaussian(key_list[1], (NQ, KVH * GROUP * HEAD), 1.0, 6.0, ((0, 4),)),
        "outlier_spans": touch_ends(jax.random.randint(key_list[2], (NOUT,), 0, ROWS_DEV // SPAN), jax.random.fold_in(key_list[2], 1), 0, (ROWS_DEV // SPAN) - 1).astype(jnp.int32),
        "start_basis": gaussian(key_list[3], (RANK, D), 1.0, 6.0, (), jnp.float32),
    }


def cholesky_pass(product):
    highest = lax.Precision.HIGHEST
    moment = jnp.dot(product.astype(jnp.float32), product.T.astype(jnp.float32), precision=highest, preferred_element_type=jnp.float32)
    factor = jnp.linalg.cholesky(moment)
    return jax.scipy.linalg.solve_triangular(factor, product, lower=True)

def group_scores(queries, key_rows):
    count_rows = key_rows.shape[0]
    scale_factor = 1.0 / math.sqrt(HEAD)
    query_heads = jnp.transpose(queries.reshape(NQ // QROWS, QROWS, KVH, GROUP, HEAD), (2, 0, 1, 3, 4))
    key_heads = jnp.transpose(key_rows.reshape(count_rows, KVH, HEAD), (1, 0, 2))

    def one_head(pairing):
        query_group, key_group = pairing
        key_float = key_group.astype(jnp.float32)

        def one_block(query_block):
            scores = jnp.einsum('qgd,cd->qgc', query_block.astype(jnp.float32), key_float, precision=lax.Precision.HIGHEST)
            return (lax.optimization_barrier(jnp.max(scores, axis=1)) * scale_factor).astype(jnp.bfloat16)
        return lax.map(one_block, query_group).reshape(NQ, count_rows)
    return lax.map(one_head, (query_heads, key_heads))

def reference(prefill_keys, queries, outlier_spans, start_basis):
    highest = lax.Precision.HIGHEST
    block_rows = math.gcd(TOKENS, 8192)

    def add_block(running, rows_block):
        rows_float = rows_block.astype(jnp.float32)
        return (running + jnp.dot(rows_float.T.astype(jnp.float32), rows_float.astype(jnp.float32), precision=highest, preferred_element_type=jnp.float32), None)
    gram_sum, unused = lax.scan(add_block, jnp.zeros((D, D), jnp.float32), prefill_keys.reshape(TOKENS // block_rows, block_rows, D))
    gram = gram_sum / TOKENS
    subspace = start_basis
    for iteration in range(ITERS):
        product = jnp.dot(subspace.astype(jnp.float32), gram.astype(jnp.float32), precision=highest, preferred_element_type=jnp.float32)
        subspace = cholesky_pass(product)
    rounded = subspace.astype(jnp.bfloat16)
    coefficients = lax.dot_general(rounded.astype(jnp.float32), prefill_keys.astype(jnp.float32), (((1,), (1,)), ((), ())), preferred_element_type=jnp.float32).astype(jnp.bfloat16)
    spanned = prefill_keys.reshape(NCHUNK, SPAN, D)
    landmarks = lax.optimization_barrier(jnp.mean(spanned.astype(jnp.float32), axis=1)).astype(jnp.bfloat16)
    owners = jnp.arange(NOUT, dtype=jnp.int32) // OUT_DEV
    global_spans = (owners * (ROWS_DEV // SPAN) + outlier_spans).astype(jnp.int32)
    picked = jnp.take(spanned, global_spans, axis=0).reshape(NOUT * SPAN, D)
    landmark_scores = group_scores(queries, landmarks)
    outlier_scores = group_scores(queries, picked)
    return (subspace, coefficients, landmark_scores, outlier_scores)
```

```python
import functools
import math

import jax
import jax.numpy as jnp
from jax import lax
from jax.experimental import pallas as pl
from jax.experimental.pallas import tpu as pltpu
from jax.sharding import PartitionSpec as P

KVH = 8
HEAD = 128
GROUP = 8
ITERS = 8
SPAN = 8
BLOCK = 32
PANEL = 8
LANES = 128
F32 = jnp.float32
BF16 = jnp.bfloat16


def split3(x):
    high = x.astype(BF16)
    rest = x - high.astype(F32)
    middle = rest.astype(BF16)
    low = (rest - middle.astype(F32)).astype(BF16)
    return high, middle, low


def dot6(left, right, contract):
    dims = (contract, ((), ()))
    rows = left[0].shape[0]
    small = lax.dot_general(left[0], right[2], dims, preferred_element_type=F32)
    two = lax.dot_general(
        jnp.concatenate(left[:2], axis=0), right[1], dims, preferred_element_type=F32
    )
    three = lax.dot_general(
        jnp.concatenate(left, axis=0), right[0], dims, preferred_element_type=F32
    )
    small = small + two[rows:] + three[2 * rows:]
    return (small + (two[:rows] + three[rows:2 * rows])) + three[:rows]


def eliminate_block(tiles, start):
    row_index = lax.broadcasted_iota(jnp.int32, (BLOCK, LANES), 0)
    tile_at, lane_at = start // LANES, start % LANES
    for panel in range(0, BLOCK, PANEL):
        lane = lane_at + panel
        columns = [
            jnp.broadcast_to(tiles[tile_at][:, lane + s:lane + s + 1], (BLOCK, LANES))
            for s in range(PANEL)
        ]
        for t in range(PANEL):
            row = panel + t
            inverse = lax.rsqrt(columns[t][row:row + 1, :])
            factor = columns[t] * inverse
            below = jnp.where(row_index > row, factor, 0.0)
            for s in range(t + 1, PANEL):
                at = panel + s
                columns[s] = columns[s] - below * factor[at:at + 1, :]
            for i in range(3):
                pivot = tiles[i][row:row + 1, :] * inverse
                tiles[i] = jnp.where(row_index == row, pivot, tiles[i] - below * pivot)
    return tiles


def inverse_factor(moment, work):
    rank = moment.shape[0]
    spare = rank - LANES
    rows = lax.broadcasted_iota(jnp.int32, (rank, LANES), 0)
    lanes = lax.broadcasted_iota(jnp.int32, (rank, LANES), 1)
    work[:, 0:LANES] = moment[:, :LANES]
    unit = jnp.where((rows == lanes + (LANES - spare)) & (lanes >= spare), 1.0, 0.0)
    work[:, LANES:2 * LANES] = jnp.where(lanes < spare, moment[:, LANES:], unit)
    work[:, 2 * LANES:] = jnp.where(rows == lanes, 1.0, 0.0)
    for start in range(0, rank, BLOCK):
        stop = start + BLOCK
        tiles = eliminate_block(
            [work[start:stop, i * LANES:(i + 1) * LANES] for i in range(3)], start
        )
        done = jnp.concatenate(tiles, axis=1)
        work[start:stop, :] = done
        if stop < rank:
            high, middle, low = split3(done)
            left = jnp.concatenate([high, middle, low, high, middle, high], axis=0)
            right = jnp.concatenate([high, high, high, middle, middle, low], axis=0)
            change = lax.dot_general(
                left[:, :2 * LANES], right, (((0,), (0,)), ((), ())), preferred_element_type=F32
            )
            work[stop:, :] = work[stop:, :] - change[stop:rank, :]
    keep = (lanes >= spare) & (lanes < 2 * spare)
    return jnp.concatenate(
        [work[:, 2 * LANES:], jnp.where(keep, work[:, LANES:2 * LANES], 0.0)], axis=1
    )


def iterate(gram, start_basis, basis, parts, spread, work):
    rank, width = basis.shape
    spare = rank - LANES
    for i, part in enumerate(split3(gram[...])):
        parts[i] = part
    for i in range(3):
        spread[i, rank + spare:, :] = jnp.zeros((LANES - 2 * spare, width), BF16)
    basis[...] = start_basis[...]

    def step(unused, carry):
        halves = split3(basis[...])
        for at in range(0, width, 2 * LANES):
            columns = pl.ds(at, 2 * LANES)
            product = dot6(halves, [parts[i, :, columns] for i in range(3)], ((1,), (0,)))
            for i, part in enumerate(split3(product)):
                spread[i, 0:rank, columns] = part
                spread[i, rank:rank + spare, columns] = part[LANES:]
        whole = [spread[i] for i in range(3)]
        moment = dot6([part[:rank] for part in whole], whole, ((1,), (1,)))
        inverse = split3(inverse_factor(moment, work))
        for at in range(0, width, 2 * LANES):
            columns = pl.ds(at, 2 * LANES)
            basis[:, columns] = dot6(
                inverse, [spread[i, :, columns] for i in range(3)], ((1,), (0,))
            )
        return carry

    lax.fori_loop(0, ITERS, step, 0)


def iterate_call(gram, start_basis):
    rank, width = start_basis.shape
    vmem = pl.BlockSpec(memory_space=pltpu.VMEM)
    return pl.pallas_call(
        iterate,
        out_shape=jax.ShapeDtypeStruct((rank, width), F32),
        in_specs=[vmem, vmem],
        out_specs=vmem,
        scratch_shapes=[
            pltpu.VMEM((3, width, width), BF16),
            pltpu.VMEM((3, 2 * LANES, width), BF16),
            pltpu.VMEM((rank, 3 * LANES), F32),
        ],
        compiler_params=pltpu.CompilerParams(vmem_limit_bytes=48 * 2**20),
        name="subspace",
    )(gram, start_basis)


def local(prefill_keys, queries, outlier_spans, start_basis):
    rows_dev = prefill_keys.shape[0]
    width = prefill_keys.shape[1]
    inverse_tokens = 1.0 / (rows_dev * lax.axis_size("kv") * lax.axis_size("seq"))
    scale_factor = 1.0 / math.sqrt(HEAD)
    spanned = prefill_keys.reshape(rows_dev // SPAN, SPAN, width)
    landmarks = jnp.mean(spanned, axis=1, dtype=jnp.float32).astype(jnp.bfloat16)
    picked = jnp.take(spanned, outlier_spans, axis=0).reshape(-1, width)
    query_count = queries.shape[0]
    query_heads = jnp.transpose(queries.reshape(query_count, KVH, GROUP, HEAD), (1, 0, 2, 3))

    def score_rows(shard_rows):
        count_rows = shard_rows.shape[0]
        key_heads = jnp.swapaxes(shard_rows.reshape(count_rows, KVH, HEAD), 0, 1)

        def one_head(pairing):
            query_group, key_group = pairing
            scores = jnp.einsum(
                "qgd,cd->qgc", query_group, key_group, preferred_element_type=jnp.float32
            )
            return jnp.max(scores, axis=1)

        return (lax.map(one_head, (query_heads, key_heads)) * scale_factor).astype(jnp.bfloat16)

    landmark_scores = score_rows(lax.all_gather(landmarks, "seq", axis=0, tiled=True))
    outlier_scores = score_rows(lax.all_gather(picked, "seq", axis=0, tiled=True))
    gram_block = lax.psum_scatter(
        lax.dot_general(
            prefill_keys, prefill_keys, (((0,), (0,)), ((), ())), preferred_element_type=jnp.float32
        )
        * inverse_tokens,
        "kv",
        scatter_dimension=0,
        tiled=True,
    )
    gram_rows = lax.psum(gram_block, "seq")
    gram = lax.all_gather(gram_rows, "kv", axis=0, tiled=True)
    subspace = iterate_call(gram, start_basis)
    rounded = subspace.astype(jnp.bfloat16)
    coefficients = lax.dot_general(
        rounded, prefill_keys, (((1,), (1,)), ((), ())), preferred_element_type=jnp.float32
    ).astype(jnp.bfloat16)
    return (subspace, coefficients, landmark_scores, outlier_scores)


def solution(mesh):
    placed = (P(("kv", "seq"), None), P("seq", None), P(("kv", "seq")), P())
    return jax.shard_map(
        local,
        mesh=mesh,
        in_specs=placed,
        out_specs=(P(), P(None, ("kv", "seq")), P(None, "seq", "kv"), P(None, "seq", "kv")),
        check_vma=False,
    )
```

```python
import functools
import math

import jax
import jax.numpy as jnp
from jax import lax
from jax.experimental import pallas as pl
from jax.experimental.pallas import tpu as pltpu
from jax.sharding import PartitionSpec as P

KVH = 8
HEAD = 128
GROUP = 8
ITERS = 8
SPAN = 8
BLOCK = 32
PANEL = 8
LANES = 128
F32 = jnp.float32
BF16 = jnp.bfloat16


def split3(x):
    high = x.astype(BF16)
    rest = x - high.astype(F32)
    middle = rest.astype(BF16)
    low = (rest - middle.astype(F32)).astype(BF16)
    return high, middle, low


def dot6(left, right, contract):
    dims = (contract, ((), ()))
    rows = left[0].shape[0]
    small = lax.dot_general(left[0], right[2], dims, preferred_element_type=F32)
    two = lax.dot_general(
        jnp.concatenate(left[:2], axis=0), right[1], dims, preferred_element_type=F32
    )
    three = lax.dot_general(
        jnp.concatenate(left, axis=0), right[0], dims, preferred_element_type=F32
    )
    small = small + two[rows:] + three[2 * rows:]
    return (small + (two[:rows] + three[rows:2 * rows])) + three[:rows]


def eliminate_block(tiles, start):
    row_index = lax.broadcasted_iota(jnp.int32, (BLOCK, LANES), 0)
    tile_at, lane_at = start // LANES, start % LANES
    for panel in range(0, BLOCK, PANEL):
        lane = lane_at + panel
        columns = [
            jnp.broadcast_to(tiles[tile_at][:, lane + s:lane + s + 1], (BLOCK, LANES))
            for s in range(PANEL)
        ]
        for t in range(PANEL):
            row = panel + t
            inverse = lax.rsqrt(columns[t][row:row + 1, :])
            factor = columns[t] * inverse
            below = jnp.where(row_index > row, factor, 0.0)
            for s in range(t + 1, PANEL):
                at = panel + s
                columns[s] = columns[s] - below * factor[at:at + 1, :]
            for i in range(3):
                pivot = tiles[i][row:row + 1, :] * inverse
                tiles[i] = jnp.where(row_index == row, pivot, tiles[i] - below * pivot)
    return tiles


def inverse_factor(moment, work):
    rank = moment.shape[0]
    spare = rank - LANES
    rows = lax.broadcasted_iota(jnp.int32, (rank, LANES), 0)
    lanes = lax.broadcasted_iota(jnp.int32, (rank, LANES), 1)
    work[:, 0:LANES] = moment[:, :LANES]
    unit = jnp.where((rows == lanes + (LANES - spare)) & (lanes >= spare), 1.0, 0.0)
    work[:, LANES:2 * LANES] = jnp.where(lanes < spare, moment[:, LANES:], unit)
    work[:, 2 * LANES:] = jnp.where(rows == lanes, 1.0, 0.0)
    for start in range(0, rank, BLOCK):
        stop = start + BLOCK
        tiles = eliminate_block(
            [work[start:stop, i * LANES:(i + 1) * LANES] for i in range(3)], start
        )
        done = jnp.concatenate(tiles, axis=1)
        work[start:stop, :] = done
        if stop < rank:
            high, middle, low = split3(done)
            left = jnp.concatenate([high, middle, low, high, middle, high], axis=0)
            right = jnp.concatenate([high, high, high, middle, middle, low], axis=0)
            change = lax.dot_general(
                left[:, :2 * LANES], right, (((0,), (0,)), ((), ())), preferred_element_type=F32
            )
            work[stop:, :] = work[stop:, :] - change[stop:rank, :]
    keep = (lanes >= spare) & (lanes < 2 * spare)
    return jnp.concatenate(
        [work[:, 2 * LANES:], jnp.where(keep, work[:, LANES:2 * LANES], 0.0)], axis=1
    )


def upper_blocks(width):
    count = width // LANES
    return [(i, j) for i in range(count) for j in range(i, count)]


def iterate(packed, start_basis, basis, parts, spread, work):
    rank, width = basis.shape
    spare = rank - LANES
    for at, (i, j) in enumerate(upper_blocks(width)):
        block = packed[at * LANES:(at + 1) * LANES, :]
        rows, columns = slice(i * LANES, (i + 1) * LANES), slice(j * LANES, (j + 1) * LANES)
        for k, part in enumerate(split3(block)):
            parts[k, rows, columns] = part
        if i != j:
            for k, part in enumerate(split3(block.T)):
                parts[k, columns, rows] = part
    for i in range(3):
        spread[i, rank + spare:, :] = jnp.zeros((LANES - 2 * spare, width), BF16)
    basis[...] = start_basis[...]

    def step(unused, carry):
        halves = split3(basis[...])
        for at in range(0, width, 2 * LANES):
            columns = pl.ds(at, 2 * LANES)
            product = dot6(halves, [parts[i, :, columns] for i in range(3)], ((1,), (0,)))
            for i, part in enumerate(split3(product)):
                spread[i, 0:rank, columns] = part
                spread[i, rank:rank + spare, columns] = part[LANES:]
        whole = [spread[i] for i in range(3)]
        moment = dot6([part[:rank] for part in whole], whole, ((1,), (1,)))
        inverse = split3(inverse_factor(moment, work))
        for at in range(0, width, 2 * LANES):
            columns = pl.ds(at, 2 * LANES)
            basis[:, columns] = dot6(
                inverse, [spread[i, :, columns] for i in range(3)], ((1,), (0,))
            )
        return carry

    lax.fori_loop(0, ITERS, step, 0)


def iterate_call(packed, start_basis):
    rank, width = start_basis.shape
    vmem = pl.BlockSpec(memory_space=pltpu.VMEM)
    return pl.pallas_call(
        iterate,
        out_shape=jax.ShapeDtypeStruct((rank, width), F32),
        in_specs=[vmem, vmem],
        out_specs=vmem,
        scratch_shapes=[
            pltpu.VMEM((3, width, width), BF16),
            pltpu.VMEM((3, 2 * LANES, width), BF16),
            pltpu.VMEM((rank, 3 * LANES), F32),
        ],
        compiler_params=pltpu.CompilerParams(vmem_limit_bytes=48 * 2**20),
        cost_estimate=pl.CostEstimate(
            flops=ITERS * 12 * rank * width * (width + 2 * rank), bytes_accessed=4 * width * width, transcendentals=0
        ),
        name="subspace",
    )(packed, start_basis)


def local_sums(inverse_tokens, spans, keys, packed, shared):
    rows_dev, width = keys.shape
    pair = 2 * LANES
    place = {at: number for number, at in enumerate(upper_blocks(width))}
    for first in range(0, width // LANES, 2):
        left = keys[:, first * LANES:first * LANES + pair]
        for other in range(first, width // LANES, 2):
            right = keys[:, other * LANES:other * LANES + pair]
            sums = lax.dot_general(
                left, right, (((0,), (0,)), ((), ())), preferred_element_type=F32
            ) * inverse_tokens
            for a in range(2):
                for b in range(2):
                    if (first + a, other + b) in place:
                        at = place[first + a, other + b] * LANES
                        packed[at:at + LANES, :] = sums[
                            a * LANES:(a + 1) * LANES, b * LANES:(b + 1) * LANES
                        ]
    used = len(place) * LANES
    if used < packed.shape[0]:
        packed[used:, :] = jnp.zeros((packed.shape[0] - used, LANES), F32)
    spans_dev = rows_dev // SPAN
    count = spans.shape[0] * SPAN
    means = pair // SPAN
    mean_row = lax.broadcasted_iota(jnp.int32, (means, pair), 0)
    mean_column = lax.broadcasted_iota(jnp.int32, (means, pair), 1)
    average = jnp.where(mean_column // SPAN == mean_row, 1.0 / SPAN, 0.0)
    pick_row = lax.broadcasted_iota(jnp.int32, (count, pair), 0)
    pick_column = lax.broadcasted_iota(jnp.int32, (count, pair), 1)
    token = pick_row % SPAN
    for e in range(spans.shape[0]):
        token = token + jnp.where(pick_row // SPAN == e, spans[e] * SPAN, 0)
    picked = jnp.zeros((count, width), F32)
    for chunk in range(rows_dev // pair):
        chosen = jnp.where(pick_column + chunk * pair == token, 1.0, 0.0)
        weights = jnp.concatenate([average, chosen], axis=0).astype(BF16)
        sums = jnp.dot(
            weights, keys[chunk * pair:(chunk + 1) * pair, :], preferred_element_type=F32
        )
        shared[chunk * means:(chunk + 1) * means, :] = sums[:means].astype(BF16)
        picked = picked + sums[means:]
    shared[spans_dev:, :] = picked.astype(BF16)


def local_call(keys, spans, inverse_tokens, packed_rows):
    rows_dev, width = keys.shape
    vmem = pl.BlockSpec(memory_space=pltpu.VMEM)
    shared_rows = rows_dev // SPAN + spans.shape[0] * SPAN
    return pl.pallas_call(
        functools.partial(local_sums, inverse_tokens),
        out_shape=(
            jax.ShapeDtypeStruct((packed_rows, LANES), F32),
            jax.ShapeDtypeStruct((shared_rows, width), BF16),
        ),
        in_specs=[pl.BlockSpec(memory_space=pltpu.SMEM), vmem],
        out_specs=(vmem, vmem),
        compiler_params=pltpu.CompilerParams(vmem_limit_bytes=48 * 2**20),
        name="local_sums",
    )(spans, keys)


def exchange_orders(sizes):
    kv = [("kv", 2**bit) for bit in range(sizes["kv"].bit_length() - 1)]
    seq = [("seq", 2**bit) for bit in range(sizes["seq"].bit_length() - 1)]
    return [
        kv[:1] + kv[1:] + seq,
        kv[:1] + kv[:0:-1] + seq,
        kv[:1] + seq + kv[1:],
    ]


def sum_devices(orders, partial, total, sums, landed, send_sem, recv_sem):
    part_rows = partial.shape[0] // len(orders)
    stages = len(orders[0])
    index = {axis: lax.axis_index(axis) for axis in ("kv", "seq")}
    side = {(axis, step): index[axis] // step % 2 for axis, step in orders[0]}
    partner = {
        (axis, step): {axis: index[axis] + (1 - 2 * side[axis, step]) * step}
        for axis, step in orders[0]
    }
    barrier = pltpu.get_barrier_semaphore()
    for bit in orders[0]:
        pl.semaphore_signal(
            barrier, inc=1, device_id=partner[bit], device_id_type=pl.DeviceIdType.MESH
        )
    pl.semaphore_wait(barrier, stages)

    def copy(source, target, number, bit):
        return pltpu.make_async_remote_copy(
            src_ref=source,
            dst_ref=target,
            send_sem=send_sem.at[number],
            recv_sem=recv_sem.at[number],
            device_id=partner[bit],
            device_id_type=pl.DeviceIdType.MESH,
        )

    sent = []
    kept = [[part * part_rows] for part in range(len(orders))]
    slot = 0
    for stage in range(stages):
        rows = part_rows >> (stage + 1)
        source = partial if stage == 0 else sums
        copies = []
        for part, order in enumerate(orders):
            bit = order[stage]
            start = kept[part][-1]
            away = pl.multiple_of(start + (1 - side[bit]) * rows, 8)
            kept[part].append(pl.multiple_of(start + side[bit] * rows, 8))
            move = copy(
                source.at[pl.ds(away, rows)],
                landed.at[pl.ds(slot, rows)],
                stage * len(orders) + part,
                bit,
            )
            move.start()
            copies.append((move, slot))
            slot += rows
        for part, (move, at) in enumerate(copies):
            mine = pl.ds(kept[part][-1], rows)
            move.wait_recv()
            target = total if stage == stages - 1 else sums
            target[mine, :] = source[mine, :] + landed[pl.ds(at, rows), :]
            sent.append(move)
    for stage in reversed(range(stages)):
        rows = part_rows >> (stage + 1)
        copies = []
        for part, order in enumerate(orders):
            mine = total.at[pl.ds(kept[part][stage + 1], rows)]
            move = copy(mine, mine, (2 * stages - 1 - stage) * len(orders) + part, order[stage])
            move.start()
            copies.append(move)
        for move in copies:
            move.wait_recv()
            sent.append(move)
    for move in sent:
        move.wait_send()


def sum_call(partial, sizes):
    orders = exchange_orders(sizes)
    vmem = pl.BlockSpec(memory_space=pltpu.VMEM)
    copies = 2 * len(orders) * len(orders[0])
    return pl.pallas_call(
        functools.partial(sum_devices, orders),
        out_shape=jax.ShapeDtypeStruct(partial.shape, F32),
        in_specs=[vmem],
        out_specs=vmem,
        scratch_shapes=[
            pltpu.VMEM(partial.shape, F32),
            pltpu.VMEM(partial.shape, F32),
            pltpu.SemaphoreType.DMA((copies,)),
            pltpu.SemaphoreType.DMA((copies,)),
        ],
        compiler_params=pltpu.CompilerParams(
            collective_id=0, has_side_effects=True, vmem_limit_bytes=48 * 2**20
        ),
        name="sum_devices",
    )(partial)


def score(scale_factor, spans_dev, queries, shared, landmark_scores, outlier_scores):
    shared_rows = landmark_scores.shape[2] // spans_dev
    each = shared.shape[0] // shared_rows

    def best(key_rows):
        largest = None
        for g in range(GROUP):
            scores = lax.dot_general(
                queries[:, g * HEAD:(g + 1) * HEAD], key_rows, (((1,), (1,)), ((), ())),
                preferred_element_type=F32,
            )
            largest = scores if largest is None else jnp.maximum(largest, scores)
        return (largest * scale_factor).astype(BF16)

    picked = []
    for s in range(shared_rows):
        at = s * each
        landmark_scores[0, :, s * spans_dev:(s + 1) * spans_dev] = best(shared[at:at + spans_dev, :])
        picked.append(shared[at + spans_dev:at + each, :])
    outlier_scores[0] = best(jnp.concatenate(picked, axis=0))


def score_call(queries, shared, spans_dev, ranks):
    count = queries.shape[0]
    rows = shared.shape[0]
    outlier_rows = rows - ranks * spans_dev
    return pl.pallas_call(
        functools.partial(score, 1.0 / math.sqrt(HEAD), spans_dev),
        grid=(KVH,),
        out_shape=(
            jax.ShapeDtypeStruct((KVH, count, ranks * spans_dev), BF16),
            jax.ShapeDtypeStruct((KVH, count, outlier_rows), BF16),
        ),
        in_specs=[
            pl.BlockSpec((count, GROUP * HEAD), lambda h: (0, h)),
            pl.BlockSpec((rows, HEAD), lambda h: (0, h)),
        ],
        out_specs=(
            pl.BlockSpec((1, count, ranks * spans_dev), lambda h: (h, 0, 0)),
            pl.BlockSpec((1, count, outlier_rows), lambda h: (h, 0, 0)),
        ),
        compiler_params=pltpu.CompilerParams(vmem_limit_bytes=32 * 2**20),
        name="scores",
    )(queries, shared)


def local(sizes, prefill_keys, queries, outlier_spans, start_basis):
    rows_dev, width = prefill_keys.shape
    devices = sizes["kv"] * sizes["seq"]
    unit = 3 * 8 * devices
    packed_rows = -(-len(upper_blocks(width)) * LANES // unit) * unit
    partial, shared = local_call(
        prefill_keys, outlier_spans, 1.0 / (rows_dev * devices), packed_rows
    )
    packed = sum_call(partial, sizes)
    shared, packed = lax.optimization_barrier((shared, packed))
    gathered = lax.all_gather(shared, "seq", axis=0, tiled=True)
    subspace = iterate_call(packed, start_basis)
    coefficients = lax.dot_general(
        subspace.astype(BF16), prefill_keys, (((1,), (1,)), ((), ())), preferred_element_type=F32
    ).astype(BF16)
    landmark_scores, outlier_scores = score_call(
        queries, gathered, rows_dev // SPAN, sizes["seq"]
    )
    return (subspace, coefficients, landmark_scores, outlier_scores)


def solution(mesh):
    placed = (P(("kv", "seq"), None), P("seq", None), P(("kv", "seq")), P())
    return jax.shard_map(
        functools.partial(local, dict(mesh.shape)),
        mesh=mesh,
        in_specs=placed,
        out_specs=(P(), P(None, ("kv", "seq")), P(None, "seq", "kv"), P(None, "seq", "kv")),
        check_vma=False,
    )
```

```python
import functools
import math

import jax
import jax.numpy as jnp
from jax import lax
from jax.experimental import pallas as pl
from jax.experimental.pallas import tpu as pltpu
from jax.sharding import PartitionSpec as P

KVH = 8
HEAD = 128
GROUP = 8
ITERS = 8
SPAN = 8
BLOCK = 32
PANEL = 8
LANES = 128
F32 = jnp.float32
BF16 = jnp.bfloat16


def split3(x):
    high = x.astype(BF16)
    rest = x - high.astype(F32)
    middle = rest.astype(BF16)
    low = (rest - middle.astype(F32)).astype(BF16)
    return high, middle, low


def dot6(left, right, contract):
    dims = (contract, ((), ()))
    rows = left[0].shape[0]
    small = lax.dot_general(left[0], right[2], dims, preferred_element_type=F32)
    two = lax.dot_general(
        jnp.concatenate(left[:2], axis=0), right[1], dims, preferred_element_type=F32
    )
    three = lax.dot_general(
        jnp.concatenate(left, axis=0), right[0], dims, preferred_element_type=F32
    )
    small = small + two[rows:] + three[2 * rows:]
    return (small + (two[:rows] + three[rows:2 * rows])) + three[:rows]


def eliminate_block(tiles, start, beside):
    row_index = lax.broadcasted_iota(jnp.int32, (BLOCK, LANES), 0)
    tile_at, lane_at = start // LANES, start % LANES
    for panel in range(0, BLOCK, PANEL):
        lane = lane_at + panel
        columns = [
            jnp.broadcast_to(tiles[tile_at][:, lane + s:lane + s + 1], (BLOCK, LANES))
            for s in range(PANEL)
        ]
        for t in range(PANEL):
            row = panel + t
            pivot = columns[t][row:row + 1, :]
            inverse = 1.0 / pivot
            below = jnp.where(row_index > row, columns[t], 0.0)
            for s in range(t + 1, PANEL):
                at = panel + s
                columns[s] = columns[s] - below * (columns[t][at:at + 1, :] * inverse)
            root = lax.rsqrt(pivot)
            for i in range(3):
                line = tiles[i][row:row + 1, :]
                tiles[i] = jnp.where(
                    row_index == row, line * root, tiles[i] - below * (line * inverse)
                )
        if panel == PANEL and beside is not None:
            beside()
    return tiles


def inverse_factor(moment, work, beside):
    rank = moment.shape[0]
    spare = rank - LANES
    rows = lax.broadcasted_iota(jnp.int32, (rank, LANES), 0)
    lanes = lax.broadcasted_iota(jnp.int32, (rank, LANES), 1)
    work[:, 0:LANES] = moment[:, :LANES]
    unit = jnp.where((rows == lanes + (LANES - spare)) & (lanes >= spare), 1.0, 0.0)
    work[:, LANES:2 * LANES] = jnp.where(lanes < spare, moment[:, LANES:], unit)
    work[:, 2 * LANES:] = jnp.where(rows == lanes, 1.0, 0.0)
    for start in range(0, rank, BLOCK):
        stop = start + BLOCK
        tiles = eliminate_block(
            [work[start:stop, i * LANES:(i + 1) * LANES] for i in range(3)],
            start,
            beside[start // BLOCK] if start // BLOCK < len(beside) else None,
        )
        done = jnp.concatenate(tiles, axis=1)
        work[start:stop, :] = done
        if stop < rank:
            high, middle, low = split3(done)
            left = jnp.concatenate([high, middle, low, high, middle, high], axis=0)
            right = jnp.concatenate([high, high, high, middle, middle, low], axis=0)
            change = lax.dot_general(
                left[:, :2 * LANES], right, (((0,), (0,)), ((), ())), preferred_element_type=F32
            )
            work[stop:, :] = work[stop:, :] - change[stop:rank, :]
    keep = (lanes >= spare) & (lanes < 2 * spare)
    return jnp.concatenate(
        [work[:, 2 * LANES:], jnp.where(keep, work[:, LANES:2 * LANES], 0.0)], axis=1
    )


def upper_blocks(width):
    count = width // LANES
    return [(i, j) for i in range(count) for j in range(i, count)]


def iterate(packed, start_basis, keys_any, basis, coefficients, parts, spread, ahead, work, keys, sem):
    fetch = pltpu.make_async_copy(keys_any, keys, sem)
    fetch.start()
    rank, width = basis.shape
    spare = rank - LANES
    for at, (i, j) in enumerate(upper_blocks(width)):
        block = packed[at * LANES:(at + 1) * LANES, :]
        rows, columns = slice(i * LANES, (i + 1) * LANES), slice(j * LANES, (j + 1) * LANES)
        for k, part in enumerate(split3(block)):
            parts[k, rows, columns] = part
        if i != j:
            for k, part in enumerate(split3(block.T)):
                parts[k, columns, rows] = part
    for i in range(3):
        unused = jnp.zeros((LANES - 2 * spare, width), BF16)
        spread[i, rank + spare:, :] = unused
        ahead[i, rank + spare:, :] = unused
    tiles = [slice(at, at + 2 * LANES) for at in range(0, width, 2 * LANES)]

    def keep(target, columns, rows):
        for i, part in enumerate(split3(rows)):
            target[i, 0:rank, columns] = part
            target[i, rank:rank + spare, columns] = part[LANES:]

    def times_gram(left, target, columns):
        keep(target, columns, dot6(left, [parts[i, :, columns] for i in range(3)], ((1,), (0,))))

    def inverse_of(whole, beside):
        moment = dot6([part[:rank] for part in whole], whole, ((1,), (1,)))
        return split3(inverse_factor(moment, work, beside))

    first = split3(start_basis[...])
    for columns in tiles:
        times_gram(first, spread, columns)

    def step(unused, carry):
        whole = [spread[i] for i in range(3)]
        top = [spread[i, 0:rank, :] for i in range(3)]
        inverse = inverse_of(
            whole, [functools.partial(times_gram, top, ahead, columns) for columns in tiles]
        )
        for columns in tiles:
            keep(
                spread,
                columns,
                dot6(inverse, [ahead[i, :, columns] for i in range(3)], ((1,), (0,))),
            )
        return carry

    lax.fori_loop(0, ITERS - 1, step, 0)
    inverse = inverse_of([spread[i] for i in range(3)], [])
    for columns in tiles:
        basis[:, columns] = dot6(
            inverse, [spread[i, :, columns] for i in range(3)], ((1,), (0,))
        )
    fetch.wait()
    rounded = basis[...].astype(BF16)
    for at in range(0, keys.shape[0], 2 * LANES):
        coefficients[:, at:at + 2 * LANES] = lax.dot_general(
            rounded, keys[at:at + 2 * LANES, :], (((1,), (1,)), ((), ())), preferred_element_type=F32
        ).astype(BF16)


def iterate_call(packed, start_basis, keys):
    rank, width = start_basis.shape
    vmem = pl.BlockSpec(memory_space=pltpu.VMEM)
    return pl.pallas_call(
        iterate,
        out_shape=(
            jax.ShapeDtypeStruct((rank, width), F32),
            jax.ShapeDtypeStruct((rank, keys.shape[0]), BF16),
        ),
        in_specs=[vmem, vmem, pl.BlockSpec(memory_space=pl.ANY)],
        out_specs=(vmem, vmem),
        scratch_shapes=[
            pltpu.VMEM((3, width, width), BF16),
            pltpu.VMEM((3, 2 * LANES, width), BF16),
            pltpu.VMEM((3, 2 * LANES, width), BF16),
            pltpu.VMEM((rank, 3 * LANES), F32),
            pltpu.VMEM(keys.shape, BF16),
            pltpu.SemaphoreType.DMA,
        ],
        compiler_params=pltpu.CompilerParams(vmem_limit_bytes=48 * 2**20),
        cost_estimate=pl.CostEstimate(
            flops=ITERS * 12 * rank * width * (width + 2 * rank), bytes_accessed=4 * width * width, transcendentals=0
        ),
        name="subspace",
    )(packed, start_basis, keys)


def local_sums(inverse_tokens, spans, keys, packed, shared):
    rows_dev, width = keys.shape
    pair = 2 * LANES
    place = {at: number for number, at in enumerate(upper_blocks(width))}
    for first in range(0, width // LANES, 2):
        left = keys[:, first * LANES:first * LANES + pair]
        for other in range(first, width // LANES, 2):
            right = keys[:, other * LANES:other * LANES + pair]
            sums = lax.dot_general(
                left, right, (((0,), (0,)), ((), ())), preferred_element_type=F32
            ) * inverse_tokens
            for a in range(2):
                for b in range(2):
                    if (first + a, other + b) in place:
                        at = place[first + a, other + b] * LANES
                        packed[at:at + LANES, :] = sums[
                            a * LANES:(a + 1) * LANES, b * LANES:(b + 1) * LANES
                        ]
    used = len(place) * LANES
    if used < packed.shape[0]:
        packed[used:, :] = jnp.zeros((packed.shape[0] - used, LANES), F32)
    spans_dev = rows_dev // SPAN
    count = spans.shape[0] * SPAN
    means = pair // SPAN
    mean_row = lax.broadcasted_iota(jnp.int32, (means, pair), 0)
    mean_column = lax.broadcasted_iota(jnp.int32, (means, pair), 1)
    average = jnp.where(mean_column // SPAN == mean_row, 1.0 / SPAN, 0.0)
    pick_row = lax.broadcasted_iota(jnp.int32, (count, pair), 0)
    pick_column = lax.broadcasted_iota(jnp.int32, (count, pair), 1)
    token = pick_row % SPAN
    for e in range(spans.shape[0]):
        token = token + jnp.where(pick_row // SPAN == e, spans[e] * SPAN, 0)
    picked = jnp.zeros((count, width), F32)
    for chunk in range(rows_dev // pair):
        chosen = jnp.where(pick_column + chunk * pair == token, 1.0, 0.0)
        weights = jnp.concatenate([average, chosen], axis=0).astype(BF16)
        sums = jnp.dot(
            weights, keys[chunk * pair:(chunk + 1) * pair, :], preferred_element_type=F32
        )
        shared[chunk * means:(chunk + 1) * means, :] = sums[:means].astype(BF16)
        picked = picked + sums[means:]
    shared[spans_dev:, :] = picked.astype(BF16)


def local_call(keys, spans, inverse_tokens, packed_rows):
    rows_dev, width = keys.shape
    vmem = pl.BlockSpec(memory_space=pltpu.VMEM)
    shared_rows = rows_dev // SPAN + spans.shape[0] * SPAN
    return pl.pallas_call(
        functools.partial(local_sums, inverse_tokens),
        out_shape=(
            jax.ShapeDtypeStruct((packed_rows, LANES), F32),
            jax.ShapeDtypeStruct((shared_rows, width), BF16),
        ),
        in_specs=[pl.BlockSpec(memory_space=pltpu.SMEM), vmem],
        out_specs=(vmem, vmem),
        compiler_params=pltpu.CompilerParams(vmem_limit_bytes=48 * 2**20),
        name="local_sums",
    )(spans, keys)


def exchange_orders(sizes):
    kv = [("kv", 2**bit) for bit in range(sizes["kv"].bit_length() - 1)]
    seq = [("seq", 2**bit) for bit in range(sizes["seq"].bit_length() - 1)]
    up = kv[:1] + kv[1:] + seq
    down = kv[:1] + kv[:0:-1] + seq
    across = kv[:1] + seq + kv[1:]
    return [(2, up), (2, down), (1, across), (2, up), (2, down)]


def sum_devices(parts, partial, total, sums, landed, send_sem, recv_sem):
    weight_rows = partial.shape[0] // sum(weight for weight, order in parts)
    bits = parts[0][1]
    stages = len(bits)
    index = {axis: lax.axis_index(axis) for axis in ("kv", "seq")}
    side = {(axis, step): index[axis] // step % 2 for axis, step in bits}
    partner = {
        (axis, step): {axis: index[axis] + (1 - 2 * side[axis, step]) * step}
        for axis, step in bits
    }
    barrier = pltpu.get_barrier_semaphore()
    for bit in bits:
        pl.semaphore_signal(
            barrier, inc=1, device_id=partner[bit], device_id_type=pl.DeviceIdType.MESH
        )
    pl.semaphore_wait(barrier, stages)

    sent = []
    kept, landings = [], []
    base = 0
    for weight, order in parts:
        kept.append([base])
        landings.append(base)
        base += weight * weight_rows

    def start(part, step):
        weight, order = parts[part]
        stage = step if step < stages else 2 * stages - 1 - step
        bit = order[stage]
        rows = weight * weight_rows >> (stage + 1)
        if step < stages:
            begin = kept[part][-1]
            away = pl.multiple_of(begin + (1 - side[bit]) * rows, 8)
            kept[part].append(pl.multiple_of(begin + side[bit] * rows, 8))
            source = (partial if step == 0 else sums).at[pl.ds(away, rows)]
            target = landed.at[pl.ds(landings[part], rows)]
        else:
            source = target = total.at[pl.ds(kept[part][stage + 1], rows)]
        number = step * len(parts) + part
        move = pltpu.make_async_remote_copy(
            src_ref=source,
            dst_ref=target,
            send_sem=send_sem.at[number],
            recv_sem=recv_sem.at[number],
            device_id=partner[bit],
            device_id_type=pl.DeviceIdType.MESH,
        )
        move.start()
        sent.append(move)
        return move

    moves = [start(part, 0) for part in range(len(parts))]
    for step in range(2 * stages):
        for part, (weight, order) in enumerate(parts):
            moves[part].wait_recv()
            if step < stages:
                rows = weight * weight_rows >> (step + 1)
                mine = pl.ds(kept[part][-1], rows)
                source = partial if step == 0 else sums
                target = total if step == stages - 1 else sums
                target[mine, :] = source[mine, :] + landed[pl.ds(landings[part], rows), :]
                landings[part] += rows
            if step < 2 * stages - 1:
                moves[part] = start(part, step + 1)
    for move in sent:
        move.wait_send()


def sum_call(partial, sizes):
    parts = exchange_orders(sizes)
    vmem = pl.BlockSpec(memory_space=pltpu.VMEM)
    copies = 2 * len(parts) * len(parts[0][1])
    return pl.pallas_call(
        functools.partial(sum_devices, parts),
        out_shape=jax.ShapeDtypeStruct(partial.shape, F32),
        in_specs=[vmem],
        out_specs=vmem,
        scratch_shapes=[
            pltpu.VMEM(partial.shape, F32),
            pltpu.VMEM(partial.shape, F32),
            pltpu.SemaphoreType.DMA((copies,)),
            pltpu.SemaphoreType.DMA((copies,)),
        ],
        compiler_params=pltpu.CompilerParams(
            collective_id=0, has_side_effects=True, vmem_limit_bytes=48 * 2**20
        ),
        name="sum_devices",
    )(partial)


def score(scale_factor, spans_dev, queries, shared, landmark_scores, outlier_scores):
    shared_rows = landmark_scores.shape[2] // spans_dev
    each = shared.shape[0] // shared_rows

    def best(key_rows):
        largest = None
        for g in range(GROUP):
            scores = lax.dot_general(
                queries[:, g * HEAD:(g + 1) * HEAD], key_rows, (((1,), (1,)), ((), ())),
                preferred_element_type=F32,
            )
            largest = scores if largest is None else jnp.maximum(largest, scores)
        return (largest * scale_factor).astype(BF16)

    picked = []
    for s in range(shared_rows):
        at = s * each
        landmark_scores[0, :, s * spans_dev:(s + 1) * spans_dev] = best(shared[at:at + spans_dev, :])
        picked.append(shared[at + spans_dev:at + each, :])
    outlier_scores[0] = best(jnp.concatenate(picked, axis=0))


def score_call(queries, shared, spans_dev, ranks):
    count = queries.shape[0]
    rows = shared.shape[0]
    outlier_rows = rows - ranks * spans_dev
    return pl.pallas_call(
        functools.partial(score, 1.0 / math.sqrt(HEAD), spans_dev),
        grid=(KVH,),
        out_shape=(
            jax.ShapeDtypeStruct((KVH, count, ranks * spans_dev), BF16),
            jax.ShapeDtypeStruct((KVH, count, outlier_rows), BF16),
        ),
        in_specs=[
            pl.BlockSpec((count, GROUP * HEAD), lambda h: (0, h)),
            pl.BlockSpec((rows, HEAD), lambda h: (0, h)),
        ],
        out_specs=(
            pl.BlockSpec((1, count, ranks * spans_dev), lambda h: (h, 0, 0)),
            pl.BlockSpec((1, count, outlier_rows), lambda h: (h, 0, 0)),
        ),
        compiler_params=pltpu.CompilerParams(vmem_limit_bytes=32 * 2**20),
        name="scores",
    )(queries, shared)


def local(sizes, prefill_keys, queries, outlier_spans, start_basis):
    rows_dev, width = prefill_keys.shape
    devices = sizes["kv"] * sizes["seq"]
    unit = sum(weight for weight, order in exchange_orders(sizes)) * 8 * devices
    packed_rows = -(-len(upper_blocks(width)) * LANES // unit) * unit
    partial, shared = local_call(
        prefill_keys, outlier_spans, 1.0 / (rows_dev * devices), packed_rows
    )
    packed = sum_call(partial, sizes)
    shared, packed = lax.optimization_barrier((shared, packed))
    gathered = lax.all_gather(shared, "seq", axis=0, tiled=True)
    subspace, coefficients = iterate_call(packed, start_basis, prefill_keys)
    landmark_scores, outlier_scores = score_call(
        queries, gathered, rows_dev // SPAN, sizes["seq"]
    )
    return (subspace, coefficients, landmark_scores, outlier_scores)


def solution(mesh):
    placed = (P(("kv", "seq"), None), P("seq", None), P(("kv", "seq")), P())
    return jax.shard_map(
        functools.partial(local, dict(mesh.shape)),
        mesh=mesh,
        in_specs=placed,
        out_specs=(P(), P(None, ("kv", "seq")), P(None, "seq", "kv"), P(None, "seq", "kv")),
        check_vma=False,
    )
```

```python
import functools
import math

import jax
import jax.numpy as jnp
from jax import lax
from jax.experimental import pallas as pl
from jax.experimental.pallas import tpu as pltpu
from jax.sharding import PartitionSpec as P

KVH = 8
HEAD = 128
GROUP = 8
ITERS = 8
SPAN = 8
BLOCK = 32
PANEL = 8
LANES = 128
F32 = jnp.float32
BF16 = jnp.bfloat16


def split3(x):
    high = x.astype(BF16)
    rest = x - high.astype(F32)
    middle = rest.astype(BF16)
    low = (rest - middle.astype(F32)).astype(BF16)
    return high, middle, low


def dot6(left, right, contract):
    dims = (contract, ((), ()))
    rows = left[0].shape[0]
    small = lax.dot_general(left[0], right[2], dims, preferred_element_type=F32)
    two = lax.dot_general(
        jnp.concatenate(left[:2], axis=0), right[1], dims, preferred_element_type=F32
    )
    three = lax.dot_general(
        jnp.concatenate(left, axis=0), right[0], dims, preferred_element_type=F32
    )
    small = small + two[rows:] + three[2 * rows:]
    return (small + (two[:rows] + three[rows:2 * rows])) + three[:rows]


def eliminate_block(tiles, start, beside):
    row_index = lax.broadcasted_iota(jnp.int32, (BLOCK, LANES), 0)
    tile_at, lane_at = start // LANES, start % LANES
    for panel in range(0, BLOCK, PANEL):
        lane = lane_at + panel
        columns = [
            jnp.broadcast_to(tiles[tile_at][:, lane + s:lane + s + 1], (BLOCK, LANES))
            for s in range(PANEL)
        ]
        for t in range(PANEL):
            row = panel + t
            pivot = columns[t][row:row + 1, :]
            inverse = 1.0 / pivot
            below = jnp.where(row_index > row, columns[t], 0.0)
            for s in range(t + 1, PANEL):
                at = panel + s
                columns[s] = columns[s] - below * (columns[t][at:at + 1, :] * inverse)
            root = lax.rsqrt(pivot)
            for i in range(3):
                line = tiles[i][row:row + 1, :]
                tiles[i] = jnp.where(
                    row_index == row, line * root, tiles[i] - below * (line * inverse)
                )
        if panel == PANEL and beside is not None:
            beside()
    return tiles


def inverse_factor(moment, work, beside):
    rank = moment.shape[0]
    spare = rank - LANES
    rows = lax.broadcasted_iota(jnp.int32, (rank, LANES), 0)
    lanes = lax.broadcasted_iota(jnp.int32, (rank, LANES), 1)
    work[:, 0:LANES] = moment[:, :LANES]
    unit = jnp.where((rows == lanes + (LANES - spare)) & (lanes >= spare), 1.0, 0.0)
    work[:, LANES:2 * LANES] = jnp.where(lanes < spare, moment[:, LANES:], unit)
    work[:, 2 * LANES:] = jnp.where(rows == lanes, 1.0, 0.0)
    for start in range(0, rank, BLOCK):
        stop = start + BLOCK
        tiles = eliminate_block(
            [work[start:stop, i * LANES:(i + 1) * LANES] for i in range(3)],
            start,
            beside[start // BLOCK] if start // BLOCK < len(beside) else None,
        )
        done = jnp.concatenate(tiles, axis=1)
        work[start:stop, :] = done
        if stop < rank:
            high, middle, low = split3(done)
            left = jnp.concatenate([high, middle, low, high, middle, high], axis=0)
            right = jnp.concatenate([high, high, high, middle, middle, low], axis=0)
            change = lax.dot_general(
                left[:, :2 * LANES], right, (((0,), (0,)), ((), ())), preferred_element_type=F32
            )
            work[stop:, :] = work[stop:, :] - change[stop:rank, :]
    keep = (lanes >= spare) & (lanes < 2 * spare)
    return jnp.concatenate(
        [work[:, 2 * LANES:], jnp.where(keep, work[:, LANES:2 * LANES], 0.0)], axis=1
    )


def upper_blocks(width):
    count = width // LANES
    return [(i, j) for i in range(count) for j in range(i, count)]


def iterate(packed, start_basis, keys_any, basis, coefficients, parts, spread, ahead, work, keys, sem):
    fetch = pltpu.make_async_copy(keys_any, keys, sem)
    fetch.start()
    rank, width = basis.shape
    spare = rank - LANES
    for at, (i, j) in enumerate(upper_blocks(width)):
        block = packed[at * LANES:(at + 1) * LANES, :]
        rows, columns = slice(i * LANES, (i + 1) * LANES), slice(j * LANES, (j + 1) * LANES)
        for k, part in enumerate(split3(block)):
            parts[k, rows, columns] = part
        if i != j:
            for k, part in enumerate(split3(block.T)):
                parts[k, columns, rows] = part
    for i in range(3):
        unused = jnp.zeros((LANES - 2 * spare, width), BF16)
        spread[i, rank + spare:, :] = unused
        ahead[i, rank + spare:, :] = unused
    tiles = [slice(at, at + 2 * LANES) for at in range(0, width, 2 * LANES)]

    def keep(target, columns, rows):
        for i, part in enumerate(split3(rows)):
            target[i, 0:rank, columns] = part
            target[i, rank:rank + spare, columns] = part[LANES:]

    def times_gram(left, target, columns):
        keep(target, columns, dot6(left, [parts[i, :, columns] for i in range(3)], ((1,), (0,))))

    def inverse_of(whole, beside):
        moment = dot6([part[:rank] for part in whole], whole, ((1,), (1,)))
        return split3(inverse_factor(moment, work, beside))

    first = split3(start_basis[...])
    for columns in tiles:
        times_gram(first, spread, columns)

    def step(unused, carry):
        whole = [spread[i] for i in range(3)]
        top = [spread[i, 0:rank, :] for i in range(3)]
        inverse = inverse_of(
            whole, [functools.partial(times_gram, top, ahead, columns) for columns in tiles]
        )
        for columns in tiles:
            keep(
                spread,
                columns,
                dot6(inverse, [ahead[i, :, columns] for i in range(3)], ((1,), (0,))),
            )
        return carry

    lax.fori_loop(0, ITERS - 1, step, 0)
    inverse = inverse_of([spread[i] for i in range(3)], [])
    for columns in tiles:
        basis[:, columns] = dot6(
            inverse, [spread[i, :, columns] for i in range(3)], ((1,), (0,))
        )
    fetch.wait()
    rounded = basis[...].astype(BF16)
    for at in range(0, keys.shape[0], 2 * LANES):
        coefficients[:, at:at + 2 * LANES] = lax.dot_general(
            rounded, keys[at:at + 2 * LANES, :], (((1,), (1,)), ((), ())), preferred_element_type=F32
        ).astype(BF16)


def iterate_call(packed, start_basis, keys):
    rank, width = start_basis.shape
    vmem = pl.BlockSpec(memory_space=pltpu.VMEM)
    return pl.pallas_call(
        iterate,
        out_shape=(
            jax.ShapeDtypeStruct((rank, width), F32),
            jax.ShapeDtypeStruct((rank, keys.shape[0]), BF16),
        ),
        in_specs=[vmem, vmem, pl.BlockSpec(memory_space=pl.ANY)],
        out_specs=(vmem, vmem),
        scratch_shapes=[
            pltpu.VMEM((3, width, width), BF16),
            pltpu.VMEM((3, 2 * LANES, width), BF16),
            pltpu.VMEM((3, 2 * LANES, width), BF16),
            pltpu.VMEM((rank, 3 * LANES), F32),
            pltpu.VMEM(keys.shape, BF16),
            pltpu.SemaphoreType.DMA,
        ],
        compiler_params=pltpu.CompilerParams(vmem_limit_bytes=48 * 2**20),
        cost_estimate=pl.CostEstimate(
            flops=ITERS * 12 * rank * width * (width + 2 * rank), bytes_accessed=4 * width * width, transcendentals=0
        ),
        name="subspace",
    )(packed, start_basis, keys)


def local_sums(inverse_tokens, spans, keys, packed, shared):
    rows_dev, width = keys.shape
    pair = 2 * LANES
    place = {at: number for number, at in enumerate(upper_blocks(width))}
    for first in range(0, width // LANES, 2):
        left = keys[:, first * LANES:first * LANES + pair]
        for other in range(first, width // LANES, 2):
            right = keys[:, other * LANES:other * LANES + pair]
            sums = lax.dot_general(
                left, right, (((0,), (0,)), ((), ())), preferred_element_type=F32
            ) * inverse_tokens
            for a in range(2):
                for b in range(2):
                    if (first + a, other + b) in place:
                        at = place[first + a, other + b] * LANES
                        packed[at:at + LANES, :] = sums[
                            a * LANES:(a + 1) * LANES, b * LANES:(b + 1) * LANES
                        ]
    used = len(place) * LANES
    if used < packed.shape[0]:
        packed[used:, :] = jnp.zeros((packed.shape[0] - used, LANES), F32)
    spans_dev = rows_dev // SPAN
    count = spans.shape[0] * SPAN
    means = pair // SPAN
    mean_row = lax.broadcasted_iota(jnp.int32, (means, pair), 0)
    mean_column = lax.broadcasted_iota(jnp.int32, (means, pair), 1)
    average = jnp.where(mean_column // SPAN == mean_row, 1.0 / SPAN, 0.0)
    pick_row = lax.broadcasted_iota(jnp.int32, (count, pair), 0)
    pick_column = lax.broadcasted_iota(jnp.int32, (count, pair), 1)
    token = pick_row % SPAN
    for e in range(spans.shape[0]):
        token = token + jnp.where(pick_row // SPAN == e, spans[e] * SPAN, 0)
    picked = jnp.zeros((count, width), F32)
    for chunk in range(rows_dev // pair):
        chosen = jnp.where(pick_column + chunk * pair == token, 1.0, 0.0)
        weights = jnp.concatenate([average, chosen], axis=0).astype(BF16)
        sums = jnp.dot(
            weights, keys[chunk * pair:(chunk + 1) * pair, :], preferred_element_type=F32
        )
        shared[chunk * means:(chunk + 1) * means, :] = sums[:means].astype(BF16)
        picked = picked + sums[means:]
    shared[spans_dev:, :] = picked.astype(BF16)


def local_call(keys, spans, inverse_tokens, packed_rows):
    rows_dev, width = keys.shape
    vmem = pl.BlockSpec(memory_space=pltpu.VMEM)
    shared_rows = rows_dev // SPAN + spans.shape[0] * SPAN
    return pl.pallas_call(
        functools.partial(local_sums, inverse_tokens),
        out_shape=(
            jax.ShapeDtypeStruct((packed_rows, LANES), F32),
            jax.ShapeDtypeStruct((shared_rows, width), BF16),
        ),
        in_specs=[pl.BlockSpec(memory_space=pltpu.SMEM), vmem],
        out_specs=(vmem, vmem),
        compiler_params=pltpu.CompilerParams(vmem_limit_bytes=48 * 2**20),
        name="local_sums",
    )(spans, keys)


def exchange_orders(sizes):
    kv = [("kv", 2**bit, 2) for bit in range(sizes["kv"].bit_length() - 1)]
    seq = [("seq", 1, sizes["seq"])]
    up = kv[:1] + kv[1:] + seq
    down = kv[:1] + kv[:0:-1] + seq
    across = kv[:1] + seq + kv[1:]
    return [(2, up), (2, down), (1, across), (2, up), (2, down)]


def copies_of(parts):
    return 2 * len(parts) * sum(size - 1 for axis, step, size in parts[0][1])


def sum_devices(parts, partial, total, sums, landed, send_sem, recv_sem):
    weight_rows = partial.shape[0] // sum(weight for weight, order in parts)
    groups = parts[0][1]
    stages = len(groups)
    index = {axis: lax.axis_index(axis) for axis in ("kv", "seq")}
    digit = {group: index[group[0]] // group[1] % group[2] for group in groups}

    def peer(group, ahead):
        axis, step, size = group
        other = (digit[group] + ahead) % size
        return other, {axis: index[axis] + (other - digit[group]) * step}

    barrier = pltpu.get_barrier_semaphore()
    count = 0
    for group in groups:
        for ahead in range(1, group[2]):
            pl.semaphore_signal(
                barrier, inc=1, device_id=peer(group, ahead)[1], device_id_type=pl.DeviceIdType.MESH
            )
            count += 1
    pl.semaphore_wait(barrier, count)

    sent = []
    kept, landings, heights = [], [], []
    base = 0
    for weight, order in parts:
        kept.append([base])
        heights.append([weight * weight_rows])
        landings.append(base)
        base += weight * weight_rows
        for axis, step, size in order:
            heights[-1].append(heights[-1][-1] // size)

    def start(part, at):
        order = parts[part][1]
        stage = at if at < stages else 2 * stages - 1 - at
        group = order[stage]
        rows = heights[part][stage + 1]
        begin = kept[part][stage]
        if at < stages:
            kept[part].append(pl.multiple_of(begin + digit[group] * rows, 8))
        moves = []
        for ahead in range(1, group[2]):
            other, device = peer(group, ahead)
            if at < stages:
                away = pl.multiple_of(begin + other * rows, 8)
                source = (partial if at == 0 else sums).at[pl.ds(away, rows)]
                target = landed.at[pl.ds(landings[part], rows)]
                landings[part] += rows
            else:
                source = target = total.at[pl.ds(kept[part][stage + 1], rows)]
            move = pltpu.make_async_remote_copy(
                src_ref=source,
                dst_ref=target,
                send_sem=send_sem.at[len(sent)],
                recv_sem=recv_sem.at[len(sent)],
                device_id=device,
                device_id_type=pl.DeviceIdType.MESH,
            )
            move.start()
            sent.append(move)
            moves.append(move)
        return moves

    moves = [start(part, 0) for part in range(len(parts))]
    for at in range(2 * stages):
        for part in range(len(parts)):
            for move in moves[part]:
                move.wait_recv()
            if at < stages:
                rows = heights[part][at + 1]
                mine = pl.ds(kept[part][-1], rows)
                source = partial if at == 0 else sums
                target = total if at == stages - 1 else sums
                value = source[mine, :]
                for back in range(len(moves[part]), 0, -1):
                    value = value + landed[pl.ds(landings[part] - back * rows, rows), :]
                target[mine, :] = value
            if at < 2 * stages - 1:
                moves[part] = start(part, at + 1)
    for move in sent:
        move.wait_send()


def sum_call(partial, sizes):
    parts = exchange_orders(sizes)
    vmem = pl.BlockSpec(memory_space=pltpu.VMEM)
    copies = copies_of(parts)
    return pl.pallas_call(
        functools.partial(sum_devices, parts),
        out_shape=jax.ShapeDtypeStruct(partial.shape, F32),
        in_specs=[vmem],
        out_specs=vmem,
        scratch_shapes=[
            pltpu.VMEM(partial.shape, F32),
            pltpu.VMEM(partial.shape, F32),
            pltpu.SemaphoreType.DMA((copies,)),
            pltpu.SemaphoreType.DMA((copies,)),
        ],
        compiler_params=pltpu.CompilerParams(
            collective_id=0, has_side_effects=True, vmem_limit_bytes=48 * 2**20
        ),
        name="sum_devices",
    )(partial)


def score(scale_factor, queries, *refs):
    shards = refs[:-3]
    landmark_scores, outlier_scores, picked = refs[-3:]
    ranks = len(shards)
    spans_dev = landmark_scores.shape[2] // ranks
    count = outlier_scores.shape[2] // ranks
    me = lax.axis_index("seq")

    def best(key_rows):
        largest = None
        for g in range(GROUP):
            scores = lax.dot_general(
                queries[:, g * HEAD:(g + 1) * HEAD], key_rows, (((1,), (1,)), ((), ())),
                preferred_element_type=F32,
            )
            largest = scores if largest is None else jnp.maximum(largest, scores)
        return (largest * scale_factor).astype(BF16)

    for back, shard in enumerate(shards):
        owner = (me - back + ranks) % ranks
        columns = pl.ds(pl.multiple_of(owner * spans_dev, LANES), spans_dev)
        landmark_scores[0, :, columns] = best(shard[:spans_dev, :])
        picked[pl.ds(pl.multiple_of(owner * count, count), count), :] = shard[spans_dev:, :]
    outlier_scores[0] = best(picked[...])


def score_call(queries, shards, spans_dev):
    rows = queries.shape[0]
    ranks = len(shards)
    each = shards[0].shape[0]
    outlier_rows = ranks * (each - spans_dev)
    return pl.pallas_call(
        functools.partial(score, 1.0 / math.sqrt(HEAD)),
        grid=(KVH,),
        out_shape=(
            jax.ShapeDtypeStruct((KVH, rows, ranks * spans_dev), BF16),
            jax.ShapeDtypeStruct((KVH, rows, outlier_rows), BF16),
        ),
        in_specs=[pl.BlockSpec((rows, GROUP * HEAD), lambda h: (0, h))]
        + [pl.BlockSpec((each, HEAD), lambda h: (0, h))] * ranks,
        out_specs=(
            pl.BlockSpec((1, rows, ranks * spans_dev), lambda h: (h, 0, 0)),
            pl.BlockSpec((1, rows, outlier_rows), lambda h: (h, 0, 0)),
        ),
        scratch_shapes=[pltpu.VMEM((outlier_rows, HEAD), BF16)],
        compiler_params=pltpu.CompilerParams(vmem_limit_bytes=58 * 2**20),
        name="scores",
    )(queries, *shards)


def local(sizes, prefill_keys, queries, outlier_spans, start_basis):
    rows_dev, width = prefill_keys.shape
    devices = sizes["kv"] * sizes["seq"]
    unit = sum(weight for weight, order in exchange_orders(sizes)) * 8 * devices
    packed_rows = -(-len(upper_blocks(width)) * LANES // unit) * unit
    partial, shared = local_call(
        prefill_keys, outlier_spans, 1.0 / (rows_dev * devices), packed_rows
    )
    packed = sum_call(partial, sizes)
    shared, packed = lax.optimization_barrier((shared, packed))
    ranks = sizes["seq"]
    shards = [shared] + [
        lax.ppermute(shared, "seq", [(s, (s + back) % ranks) for s in range(ranks)])
        for back in range(1, ranks)
    ]
    subspace, coefficients = iterate_call(packed, start_basis, prefill_keys)
    landmark_scores, outlier_scores = score_call(queries, shards, rows_dev // SPAN)
    return (subspace, coefficients, landmark_scores, outlier_scores)


def solution(mesh):
    placed = (P(("kv", "seq"), None), P("seq", None), P(("kv", "seq")), P())
    return jax.shard_map(
        functools.partial(local, dict(mesh.shape)),
        mesh=mesh,
        in_specs=placed,
        out_specs=(P(), P(None, ("kv", "seq")), P(None, "seq", "kv"), P(None, "seq", "kv")),
        check_vma=False,
    )
```

```python
import functools
import math

import jax
import jax.numpy as jnp
from jax import lax
from jax.experimental import pallas as pl
from jax.experimental.pallas import tpu as pltpu
from jax.sharding import PartitionSpec as P

KVH = 8
HEAD = 128
GROUP = 8
ITERS = 8
SPAN = 8
BLOCK = 32
PANEL = 8
LANES = 128
F32 = jnp.float32
BF16 = jnp.bfloat16


def split3(x):
    high = x.astype(BF16)
    rest = x - high.astype(F32)
    middle = rest.astype(BF16)
    low = (rest - middle.astype(F32)).astype(BF16)
    return high, middle, low


def dot6(left, right, contract):
    dims = (contract, ((), ()))
    rows = left[0].shape[0]
    small = lax.dot_general(left[0], right[2], dims, preferred_element_type=F32)
    two = lax.dot_general(
        jnp.concatenate(left[:2], axis=0), right[1], dims, preferred_element_type=F32
    )
    three = lax.dot_general(
        jnp.concatenate(left, axis=0), right[0], dims, preferred_element_type=F32
    )
    small = small + two[rows:] + three[2 * rows:]
    return (small + (two[:rows] + three[rows:2 * rows])) + three[:rows]


def eliminate_block(tiles, start, beside):
    row_index = lax.broadcasted_iota(jnp.int32, (BLOCK, LANES), 0)
    tile_at, lane_at = start // LANES, start % LANES
    for panel in range(0, BLOCK, PANEL):
        lane = lane_at + panel
        columns = [
            jnp.broadcast_to(tiles[tile_at][:, lane + s:lane + s + 1], (BLOCK, LANES))
            for s in range(PANEL)
        ]
        for t in range(PANEL):
            row = panel + t
            pivot = columns[t][row:row + 1, :]
            inverse = 1.0 / pivot
            below = jnp.where(row_index > row, columns[t], 0.0)
            for s in range(t + 1, PANEL):
                at = panel + s
                columns[s] = columns[s] - below * (columns[t][at:at + 1, :] * inverse)
            root = lax.rsqrt(pivot)
            for i in range(3):
                line = tiles[i][row:row + 1, :]
                tiles[i] = jnp.where(
                    row_index == row, line * root, tiles[i] - below * (line * inverse)
                )
        if panel == PANEL and beside is not None:
            beside()
    return tiles


def inverse_factor(moment, work, beside):
    rank = moment.shape[0]
    spare = rank - LANES
    rows = lax.broadcasted_iota(jnp.int32, (rank, LANES), 0)
    lanes = lax.broadcasted_iota(jnp.int32, (rank, LANES), 1)
    work[:, 0:LANES] = moment[:, :LANES]
    unit = jnp.where((rows == lanes + (LANES - spare)) & (lanes >= spare), 1.0, 0.0)
    work[:, LANES:2 * LANES] = jnp.where(lanes < spare, moment[:, LANES:], unit)
    work[:, 2 * LANES:] = jnp.where(rows == lanes, 1.0, 0.0)
    for start in range(0, rank, BLOCK):
        stop = start + BLOCK
        tiles = eliminate_block(
            [work[start:stop, i * LANES:(i + 1) * LANES] for i in range(3)],
            start,
            beside[start // BLOCK] if start // BLOCK < len(beside) else None,
        )
        done = jnp.concatenate(tiles, axis=1)
        work[start:stop, :] = done
        if stop < rank:
            high, middle, low = split3(done)
            left = jnp.concatenate([high, middle, low, high, middle, high], axis=0)
            right = jnp.concatenate([high, high, high, middle, middle, low], axis=0)
            change = lax.dot_general(
                left[:, :2 * LANES], right, (((0,), (0,)), ((), ())), preferred_element_type=F32
            )
            work[stop:, :] = work[stop:, :] - change[stop:rank, :]
    keep = (lanes >= spare) & (lanes < 2 * spare)
    return jnp.concatenate(
        [work[:, 2 * LANES:], jnp.where(keep, work[:, LANES:2 * LANES], 0.0)], axis=1
    )


def upper_blocks(width):
    count = width // LANES
    return [(i, j) for i in range(count) for j in range(i, count)]


def iterate(packed, start_basis, keys_any, basis, coefficients, parts, spread, ahead, work, keys, sem):
    fetch = pltpu.make_async_copy(keys_any, keys, sem)
    fetch.start()
    rank, width = basis.shape
    spare = rank - LANES
    for at, (i, j) in enumerate(upper_blocks(width)):
        block = packed[at * LANES:(at + 1) * LANES, :]
        rows, columns = slice(i * LANES, (i + 1) * LANES), slice(j * LANES, (j + 1) * LANES)
        for k, part in enumerate(split3(block)):
            parts[k, rows, columns] = part
        if i != j:
            for k, part in enumerate(split3(block.T)):
                parts[k, columns, rows] = part
    for i in range(3):
        unused = jnp.zeros((LANES - 2 * spare, width), BF16)
        spread[i, rank + spare:, :] = unused
        ahead[i, rank + spare:, :] = unused
    tiles = [slice(at, at + 2 * LANES) for at in range(0, width, 2 * LANES)]

    def keep(target, columns, rows):
        for i, part in enumerate(split3(rows)):
            target[i, 0:rank, columns] = part
            target[i, rank:rank + spare, columns] = part[LANES:]

    def times_gram(left, target, columns):
        keep(target, columns, dot6(left, [parts[i, :, columns] for i in range(3)], ((1,), (0,))))

    def inverse_of(whole, beside):
        moment = dot6([part[:rank] for part in whole], whole, ((1,), (1,)))
        return split3(inverse_factor(moment, work, beside))

    first = split3(start_basis[...])
    for columns in tiles:
        times_gram(first, spread, columns)

    def step(unused, carry):
        whole = [spread[i] for i in range(3)]
        top = [spread[i, 0:rank, :] for i in range(3)]
        inverse = inverse_of(
            whole, [functools.partial(times_gram, top, ahead, columns) for columns in tiles]
        )
        for columns in tiles:
            keep(
                spread,
                columns,
                dot6(inverse, [ahead[i, :, columns] for i in range(3)], ((1,), (0,))),
            )
        return carry

    lax.fori_loop(0, ITERS - 1, step, 0)
    inverse = inverse_of([spread[i] for i in range(3)], [])
    for columns in tiles:
        basis[:, columns] = dot6(
            inverse, [spread[i, :, columns] for i in range(3)], ((1,), (0,))
        )
    fetch.wait()
    rounded = basis[...].astype(BF16)
    for at in range(0, keys.shape[0], 2 * LANES):
        coefficients[:, at:at + 2 * LANES] = lax.dot_general(
            rounded, keys[at:at + 2 * LANES, :], (((1,), (1,)), ((), ())), preferred_element_type=F32
        ).astype(BF16)


def iterate_call(packed, start_basis, keys):
    rank, width = start_basis.shape
    vmem = pl.BlockSpec(memory_space=pltpu.VMEM)
    return pl.pallas_call(
        iterate,
        out_shape=(
            jax.ShapeDtypeStruct((rank, width), F32),
            jax.ShapeDtypeStruct((rank, keys.shape[0]), BF16),
        ),
        in_specs=[vmem, vmem, pl.BlockSpec(memory_space=pl.ANY)],
        out_specs=(vmem, vmem),
        scratch_shapes=[
            pltpu.VMEM((3, width, width), BF16),
            pltpu.VMEM((3, 2 * LANES, width), BF16),
            pltpu.VMEM((3, 2 * LANES, width), BF16),
            pltpu.VMEM((rank, 3 * LANES), F32),
            pltpu.VMEM(keys.shape, BF16),
            pltpu.SemaphoreType.DMA,
        ],
        compiler_params=pltpu.CompilerParams(vmem_limit_bytes=48 * 2**20),
        cost_estimate=pl.CostEstimate(
            flops=ITERS * 12 * rank * width * (width + 2 * rank), bytes_accessed=4 * width * width, transcendentals=0
        ),
        name="subspace",
    )(packed, start_basis, keys)


def local_sums(inverse_tokens, spans, keys, packed, shared):
    rows_dev, width = keys.shape
    pair = 2 * LANES
    place = {at: number for number, at in enumerate(upper_blocks(width))}
    for first in range(0, width // LANES, 2):
        left = keys[:, first * LANES:first * LANES + pair]
        for other in range(first, width // LANES, 2):
            right = keys[:, other * LANES:other * LANES + pair]
            sums = lax.dot_general(
                left, right, (((0,), (0,)), ((), ())), preferred_element_type=F32
            ) * inverse_tokens
            for a in range(2):
                for b in range(2):
                    if (first + a, other + b) in place:
                        at = place[first + a, other + b] * LANES
                        packed[at:at + LANES, :] = sums[
                            a * LANES:(a + 1) * LANES, b * LANES:(b + 1) * LANES
                        ]
    used = len(place) * LANES
    if used < packed.shape[0]:
        packed[used:, :] = jnp.zeros((packed.shape[0] - used, LANES), F32)
    spans_dev = rows_dev // SPAN
    count = spans.shape[0] * SPAN
    means = pair // SPAN
    mean_row = lax.broadcasted_iota(jnp.int32, (means, pair), 0)
    mean_column = lax.broadcasted_iota(jnp.int32, (means, pair), 1)
    average = jnp.where(mean_column // SPAN == mean_row, 1.0 / SPAN, 0.0)
    pick_row = lax.broadcasted_iota(jnp.int32, (count, pair), 0)
    pick_column = lax.broadcasted_iota(jnp.int32, (count, pair), 1)
    token = pick_row % SPAN
    for e in range(spans.shape[0]):
        token = token + jnp.where(pick_row // SPAN == e, spans[e] * SPAN, 0)
    picked = jnp.zeros((count, width), F32)
    for chunk in range(rows_dev // pair):
        chosen = jnp.where(pick_column + chunk * pair == token, 1.0, 0.0)
        weights = jnp.concatenate([average, chosen], axis=0).astype(BF16)
        sums = jnp.dot(
            weights, keys[chunk * pair:(chunk + 1) * pair, :], preferred_element_type=F32
        )
        shared[chunk * means:(chunk + 1) * means, :] = sums[:means].astype(BF16)
        picked = picked + sums[means:]
    shared[spans_dev:, :] = picked.astype(BF16)


def local_call(keys, spans, inverse_tokens, packed_rows):
    rows_dev, width = keys.shape
    vmem = pl.BlockSpec(memory_space=pltpu.VMEM)
    shared_rows = rows_dev // SPAN + spans.shape[0] * SPAN
    return pl.pallas_call(
        functools.partial(local_sums, inverse_tokens),
        out_shape=(
            jax.ShapeDtypeStruct((packed_rows, LANES), F32),
            jax.ShapeDtypeStruct((shared_rows, width), BF16),
        ),
        in_specs=[pl.BlockSpec(memory_space=pltpu.SMEM), vmem],
        out_specs=(vmem, vmem),
        compiler_params=pltpu.CompilerParams(vmem_limit_bytes=48 * 2**20),
        name="local_sums",
    )(spans, keys)


def exchange_orders(sizes):
    kv = [("kv", 2**bit, 2) for bit in range(sizes["kv"].bit_length() - 1)]
    seq = [("seq", 1, sizes["seq"])]
    up = kv[:1] + kv[1:] + seq
    down = kv[:1] + kv[:0:-1] + seq
    across = kv[:1] + seq + kv[1:]
    return [(4, up), (4, down), (1, across)]


def copies_of(parts):
    return 2 * len(parts) * sum(size - 1 for axis, step, size in parts[0][1])


def sum_devices(parts, partial, total, sums, landed, send_sem, recv_sem):
    weight_rows = partial.shape[0] // sum(weight for weight, order in parts)
    groups = parts[0][1]
    stages = len(groups)
    index = {axis: lax.axis_index(axis) for axis in ("kv", "seq")}
    digit = {group: index[group[0]] // group[1] % group[2] for group in groups}

    def peer(group, ahead):
        axis, step, size = group
        other = (digit[group] + ahead) % size
        return other, {axis: index[axis] + (other - digit[group]) * step}

    barrier = pltpu.get_barrier_semaphore()
    count = 0
    for group in groups:
        for ahead in range(1, group[2]):
            pl.semaphore_signal(
                barrier, inc=1, device_id=peer(group, ahead)[1], device_id_type=pl.DeviceIdType.MESH
            )
            count += 1
    pl.semaphore_wait(barrier, count)

    sent = []
    kept, landings, heights = [], [], []
    base = 0
    for weight, order in parts:
        kept.append([base])
        heights.append([weight * weight_rows])
        landings.append(base)
        base += weight * weight_rows
        for axis, step, size in order:
            heights[-1].append(heights[-1][-1] // size)

    def start(part, at):
        order = parts[part][1]
        stage = at if at < stages else 2 * stages - 1 - at
        group = order[stage]
        rows = heights[part][stage + 1]
        begin = kept[part][stage]
        if at < stages:
            kept[part].append(pl.multiple_of(begin + digit[group] * rows, 8))
        moves = []
        for ahead in range(1, group[2]):
            other, device = peer(group, ahead)
            if at < stages:
                away = pl.multiple_of(begin + other * rows, 8)
                source = (partial if at == 0 else sums).at[pl.ds(away, rows)]
                target = landed.at[pl.ds(landings[part], rows)]
                landings[part] += rows
            else:
                source = target = total.at[pl.ds(kept[part][stage + 1], rows)]
            move = pltpu.make_async_remote_copy(
                src_ref=source,
                dst_ref=target,
                send_sem=send_sem.at[len(sent)],
                recv_sem=recv_sem.at[len(sent)],
                device_id=device,
                device_id_type=pl.DeviceIdType.MESH,
            )
            move.start()
            sent.append(move)
            moves.append(move)
        return moves

    moves = [start(part, 0) for part in range(len(parts))]
    for at in range(2 * stages):
        for part in range(len(parts)):
            for move in moves[part]:
                move.wait_recv()
            if at < stages:
                rows = heights[part][at + 1]
                mine = pl.ds(kept[part][-1], rows)
                source = partial if at == 0 else sums
                target = total if at == stages - 1 else sums
                value = source[mine, :]
                for back in range(len(moves[part]), 0, -1):
                    value = value + landed[pl.ds(landings[part] - back * rows, rows), :]
                target[mine, :] = value
            if at < 2 * stages - 1:
                moves[part] = start(part, at + 1)
    for move in sent:
        move.wait_send()


def sum_call(partial, sizes):
    parts = exchange_orders(sizes)
    vmem = pl.BlockSpec(memory_space=pltpu.VMEM)
    copies = copies_of(parts)
    return pl.pallas_call(
        functools.partial(sum_devices, parts),
        out_shape=jax.ShapeDtypeStruct(partial.shape, F32),
        in_specs=[vmem],
        out_specs=vmem,
        scratch_shapes=[
            pltpu.VMEM(partial.shape, F32),
            pltpu.VMEM(partial.shape, F32),
            pltpu.SemaphoreType.DMA((copies,)),
            pltpu.SemaphoreType.DMA((copies,)),
        ],
        compiler_params=pltpu.CompilerParams(
            collective_id=0, has_side_effects=True, vmem_limit_bytes=48 * 2**20
        ),
        name="sum_devices",
    )(partial)


def score(scale_factor, queries, *refs):
    shards = refs[:-3]
    landmark_scores, outlier_scores, picked = refs[-3:]
    ranks = len(shards)
    spans_dev = landmark_scores.shape[2] // ranks
    count = outlier_scores.shape[2] // ranks
    me = lax.axis_index("seq")

    def best(key_rows):
        largest = None
        for g in range(GROUP):
            scores = lax.dot_general(
                queries[:, g * HEAD:(g + 1) * HEAD], key_rows, (((1,), (1,)), ((), ())),
                preferred_element_type=F32,
            )
            largest = scores if largest is None else jnp.maximum(largest, scores)
        return (largest * scale_factor).astype(BF16)

    for back, shard in enumerate(shards):
        owner = (me - back + ranks) % ranks
        columns = pl.ds(pl.multiple_of(owner * spans_dev, LANES), spans_dev)
        landmark_scores[0, :, columns] = best(shard[:spans_dev, :])
        picked[pl.ds(pl.multiple_of(owner * count, count), count), :] = shard[spans_dev:, :]
    outlier_scores[0] = best(picked[...])


def score_call(queries, shards, spans_dev):
    rows = queries.shape[0]
    ranks = len(shards)
    each = shards[0].shape[0]
    outlier_rows = ranks * (each - spans_dev)
    return pl.pallas_call(
        functools.partial(score, 1.0 / math.sqrt(HEAD)),
        grid=(KVH,),
        out_shape=(
            jax.ShapeDtypeStruct((KVH, rows, ranks * spans_dev), BF16),
            jax.ShapeDtypeStruct((KVH, rows, outlier_rows), BF16),
        ),
        in_specs=[pl.BlockSpec((rows, GROUP * HEAD), lambda h: (0, h))]
        + [pl.BlockSpec((each, HEAD), lambda h: (0, h))] * ranks,
        out_specs=(
            pl.BlockSpec((1, rows, ranks * spans_dev), lambda h: (h, 0, 0)),
            pl.BlockSpec((1, rows, outlier_rows), lambda h: (h, 0, 0)),
        ),
        scratch_shapes=[pltpu.VMEM((outlier_rows, HEAD), BF16)],
        compiler_params=pltpu.CompilerParams(vmem_limit_bytes=58 * 2**20),
        name="scores",
    )(queries, *shards)


def local(sizes, prefill_keys, queries, outlier_spans, start_basis):
    rows_dev, width = prefill_keys.shape
    devices = sizes["kv"] * sizes["seq"]
    unit = sum(weight for weight, order in exchange_orders(sizes)) * 8 * devices
    packed_rows = -(-len(upper_blocks(width)) * LANES // unit) * unit
    partial, shared = local_call(
        prefill_keys, outlier_spans, 1.0 / (rows_dev * devices), packed_rows
    )
    packed = sum_call(partial, sizes)
    shared, packed = lax.optimization_barrier((shared, packed))
    ranks = sizes["seq"]
    shards = [shared] + [
        lax.ppermute(shared, "seq", [(s, (s + back) % ranks) for s in range(ranks)])
        for back in range(1, ranks)
    ]
    subspace, coefficients = iterate_call(packed, start_basis, prefill_keys)
    landmark_scores, outlier_scores = score_call(queries, shards, rows_dev // SPAN)
    return (subspace, coefficients, landmark_scores, outlier_scores)


def solution(mesh):
    placed = (P(("kv", "seq"), None), P("seq", None), P(("kv", "seq")), P())
    return jax.shard_map(
        functools.partial(local, dict(mesh.shape)),
        mesh=mesh,
        in_specs=placed,
        out_specs=(P(), P(None, ("kv", "seq")), P(None, "seq", "kv"), P(None, "seq", "kv")),
        check_vma=False,
    )
```
